32 devices in a mesh: sec: 4 (over y, core), cp: 8 (over z, x).
Axes of the slice: x: 2, y: 2, z: 4, core: 2. Of those that a mesh axis runs over, the one named last changes fastest.
Arguments:
- projected: bfloat16 [4096, 10240], P(('sec', 'cp')), may hold values from -6 to 6
- conv_weight: float32 [4, 10240], replicated, may hold values from -3 to 3
- conv_bias: float32 [10240], replicated, may hold values from -3 to 3
- step_size: bfloat16 [4096, 128], P(('sec', 'cp')), may hold values from 0 to 1
- log_decay: bfloat16 [4096, 128], P(('sec', 'cp')), may hold values from -1 to 0
- skip_gain: float32 [128], replicated, may hold values from 0.5 to 1.5
Outputs:
- ssd_out: bfloat16 [4096, 8192], P(('sec', 'cp'))
The draws below stay inside these ranges and needn't reach their ends.
All inputs are finite; a program needn't handle non-finite values.
Results may differ from the reference program's by a relative error of at most 0.0034.
Values may be sent and summed in bfloat16 or wider, within the bound.
A program may use at most 64 MiB of HBM per device.

```python
import math
import jax
import jax.numpy as jnp
from jax import lax

HEAD_COUNT = 128
P_SIZE = 64
N = 128
G = 8
BLOCK = 256
KERNEL = 4
CH = 10240
SEQUENCE_TOKENS = 4096


def decay_and_steps(key):
    head_key = jax.random.fold_in(key, 101)
    fast_key = jax.random.fold_in(key, 102)
    slow_key = jax.random.fold_in(key, 103)
    rough_key = jax.random.fold_in(key, 104)
    spike_random_key = jax.random.fold_in(key, 105)
    amount_random_key = jax.random.fold_in(key, 106)
    step_key = jax.random.fold_in(key, 107)
    fast_share = 0.4
    head_draw = jax.random.uniform(head_key, (HEAD_COUNT,), jnp.float32)
    fast_rates = jnp.exp(jax.random.uniform(fast_key, (HEAD_COUNT,), jnp.float32, math.log(1.0 / 50.0), math.log(1.0 / 30.0)))
    slow_rates = jnp.exp(jax.random.uniform(slow_key, (HEAD_COUNT,), jnp.float32, math.log(0.2), math.log(0.8))) / SEQUENCE_TOKENS
    baseline_rate = jnp.where(head_draw < fast_share, fast_rates, slow_rates)
    jaggedness = jnp.exp(jax.random.uniform(rough_key, (SEQUENCE_TOKENS, HEAD_COUNT), jnp.float32, math.log(0.5), math.log(2.0)))
    spike_mask = jax.random.uniform(spike_random_key, (SEQUENCE_TOKENS, HEAD_COUNT), jnp.float32) < 2.0 / SEQUENCE_TOKENS
    spike_magnitude = jax.random.uniform(amount_random_key, (SEQUENCE_TOKENS, HEAD_COUNT), jnp.float32, 0.22, 0.69)
    combined_rate = baseline_rate[None, :] * jaggedness + jnp.where(spike_mask, spike_magnitude, 0.0)
    step_values = jnp.sqrt(baseline_rate / 8.0)[None, :] * jnp.exp(jax.random.uniform(step_key, (SEQUENCE_TOKENS, HEAD_COUNT), jnp.float32, math.log(0.5), math.log(2.0)))
    return (-combined_rate, step_values)


def draw_log_decay(key, part):
    return decay_and_steps(key)[0].astype(jnp.bfloat16)


def draw_step_size(key, part):
    return decay_and_steps(key)[1].astype(jnp.bfloat16)


def level_of(stream_key, shape, pieces, smallest, high):
    factor_of = 1.0
    for axis_at, blocks in pieces:
        steps = jax.random.uniform(jax.random.fold_in(jax.random.fold_in(stream_key, 6), axis_at), (blocks,), jnp.float32, smallest / len(pieces), high / len(pieces))
        factor_of = factor_of * jnp.repeat(jnp.exp(steps), shape[axis_at] // blocks).reshape((-1,) + (1,) * (len(shape) - 1 - axis_at))
    return factor_of


def bell_draw(key, dims, scale, most, pieces=(), kind=jnp.bfloat16):
    values = scale * jax.random.normal(key, dims, jnp.float32)
    if pieces:
        values = values * level_of(key, dims, pieces, -0.22, 0.18)
    return jnp.clip(values, -most, most).astype(kind)


def setup_inputs(seed: int = 0) -> dict:
    keys = jax.random.split(jax.random.key(seed), 7)
    projected = bell_draw(keys[0], (SEQUENCE_TOKENS, CH), 1.0, 6.0, ((0, 32),))
    conv_weight = bell_draw(keys[1], (KERNEL, CH), KERNEL ** -0.5, 3.0, (), jnp.float32)
    conv_bias = bell_draw(keys[2], (CH,), 0.5, 3.0, (), jnp.float32)
    step_size = draw_step_size(jax.random.fold_in(keys[6], 71), 0)
    log_decay = draw_log_decay(jax.random.fold_in(keys[6], 71), 0)
    skip_gain = jnp.clip(jax.random.uniform(keys[5], (HEAD_COUNT,), jnp.float32, 0.5, 1.5), 0.5, 1.5)
    return {"projected": projected, "conv_weight": conv_weight, "conv_bias": conv_bias, "step_size": step_size, "log_decay": log_decay, "skip_gain": skip_gain}


def causal_conv(columns, weights, biases):
    padded = jnp.concatenate([jnp.zeros((KERNEL - 1, columns.shape[1]), columns.dtype), columns], 0)
    length = columns.shape[0]
    summed = biases[None, :] + weights[0][None, :] * padded[0:length].astype(jnp.float32)
    for offset in range(1, KERNEL):
        summed = summed + weights[offset][None, :] * padded[offset:offset + length].astype(jnp.float32)
    return jax.nn.silu(summed).astype(jnp.bfloat16)


def head_output(head_index, projected, conv_weight, conv_bias, step_size, log_decay, skip_gain):
    group_index = head_index // (HEAD_COUNT // G)
    start_x = head_index * P_SIZE
    start_b = HEAD_COUNT * P_SIZE + group_index * N
    start_c = HEAD_COUNT * P_SIZE + G * N + group_index * N
    columns = jnp.concatenate([lax.dynamic_slice_in_dim(projected, start_x, P_SIZE, 1),
                               lax.dynamic_slice_in_dim(projected, start_b, N, 1),
                               lax.dynamic_slice_in_dim(projected, start_c, N, 1)], 1)
    weights = jnp.concatenate([lax.dynamic_slice_in_dim(conv_weight, start_x, P_SIZE, 1),
                               lax.dynamic_slice_in_dim(conv_weight, start_b, N, 1),
                               lax.dynamic_slice_in_dim(conv_weight, start_c, N, 1)], 1)
    biases = jnp.concatenate([lax.dynamic_slice_in_dim(conv_bias, start_x, P_SIZE, 0),
                              lax.dynamic_slice_in_dim(conv_bias, start_b, N, 0),
                              lax.dynamic_slice_in_dim(conv_bias, start_c, N, 0)], 0)
    convolved = causal_conv(columns, weights, biases)
    blocks = SEQUENCE_TOKENS // BLOCK
    values = convolved[:, :P_SIZE].reshape(blocks, BLOCK, P_SIZE)
    keys_b = convolved[:, P_SIZE:P_SIZE + N].reshape(blocks, BLOCK, N)
    query_c = convolved[:, P_SIZE + N:].reshape(blocks, BLOCK, N)
    decay_log = lax.dynamic_slice_in_dim(log_decay, head_index, 1, 1)[:, 0].astype(jnp.float32).reshape(blocks, BLOCK)
    steps_f = lax.dynamic_slice_in_dim(step_size, head_index, 1, 1)[:, 0].astype(jnp.float32).reshape(blocks, BLOCK)
    running = jnp.cumsum(decay_log, axis=1)
    block_end = running[:, -1:]
    weighted_b = (keys_b.astype(jnp.float32) * (jnp.exp(block_end - running) * steps_f)[:, :, None]).astype(jnp.bfloat16)
    block_states = jnp.einsum('csn,csp->cnp', weighted_b.astype(jnp.float32), values.astype(jnp.float32))
    block_gain = jnp.exp(block_end[:, 0])

    def advance(carried, inputs_now):
        add_state, gain_now = inputs_now
        return gain_now * carried + add_state, carried

    _, entering = lax.scan(advance, jnp.zeros((N, P_SIZE), jnp.float32), (block_states, block_gain))
    causal_mask = lax.broadcasted_iota(jnp.int32, (BLOCK, BLOCK), 0) >= lax.broadcasted_iota(jnp.int32, (BLOCK, BLOCK), 1)
    scores = jnp.einsum('ctn,csn->cts', query_c.astype(jnp.float32), keys_b.astype(jnp.float32))
    log_gap = jnp.where(causal_mask[None], running[:, :, None] - running[:, None, :], -jnp.inf)
    mix_weights = (scores * jnp.exp(log_gap) * steps_f[:, None, :]).astype(jnp.bfloat16)
    within = jnp.einsum('cts,csp->ctp', mix_weights.astype(jnp.float32), values.astype(jnp.float32))
    carried_part = jnp.einsum('ctn,cnp->ctp', query_c.astype(jnp.float32), entering,
                              precision=lax.Precision.HIGHEST) * jnp.exp(running)[:, :, None]
    skip_here = lax.dynamic_slice_in_dim(skip_gain, head_index, 1, 0)
    result = (within + carried_part + skip_here * values.astype(jnp.float32)).astype(jnp.bfloat16)
    return result.reshape(SEQUENCE_TOKENS, P_SIZE)


def reference(projected, conv_weight, conv_bias, step_size, log_decay, skip_gain):
    def one_head(head_index, buffer):
        head_index = jnp.asarray(head_index).astype(jnp.int32)
        result = head_output(head_index, projected, conv_weight, conv_bias, step_size, log_decay, skip_gain)
        return lax.dynamic_update_slice_in_dim(buffer, result, head_index * P_SIZE, 1)

    return lax.fori_loop(0, HEAD_COUNT, one_head, jnp.zeros((SEQUENCE_TOKENS, HEAD_COUNT * P_SIZE), jnp.bfloat16))
```

```python
import functools
import jax
import jax.numpy as jnp
from jax import lax
from jax.experimental import pallas as pl
from jax.experimental.pallas import tpu as pltpu
from jax.sharding import PartitionSpec as P

HEAD_COUNT = 128
P_SIZE = 64
N = 128
G = 8
KERNEL = 4
GROUP_HEADS = HEAD_COUNT // G
GROUP_COLS = GROUP_HEADS * P_SIZE
WIDTH_X = HEAD_COUNT * P_SIZE
RIM = 8
VMEM_LIMIT = 48 * 1024 * 1024


def passed_along(value, axis, steps):
    count = lax.axis_size(axis)
    return lax.ppermute(value, axis, [(source, source + steps) for source in range(count - steps)])


def conv_silu(block_ref, rim_ref, weight_ref, bias_ref):
    now = block_ref[...].astype(jnp.float32)
    rim = rim_ref[...].astype(jnp.float32)
    row = lax.broadcasted_iota(jnp.int32, rim.shape, 0)
    total = bias_ref[...] + weight_ref[KERNEL - 1 : KERNEL, :] * now
    for back in range(1, KERNEL):
        moved = pltpu.roll(now, back, 0)
        top = jnp.where(row < back, pltpu.roll(rim, back, 0), moved[:RIM])
        moved = jnp.concatenate([top, moved[RIM:]], 0)
        total = total + weight_ref[KERNEL - 1 - back : KERNEL - back, :] * moved
    return (total / (1.0 + jnp.exp(-total))).astype(jnp.bfloat16)


def spread(columns, pair):
    rows = columns.shape[0]
    lane = lax.broadcasted_iota(jnp.int32, (rows, 2 * P_SIZE), 1)
    return jnp.where(lane < P_SIZE, columns[:, 2 * pair : 2 * pair + 1], columns[:, 2 * pair + 1 : 2 * pair + 2])


def conv_state_kernel(
    px, pb, pc, rx, rb, rc, wx, wb, wc, bx, bb, bc, run_ref, step_ref,
    x_out, b_out, c_out, state_out,
):
    x = conv_silu(px, rx, wx, bx)
    b = conv_silu(pb, rb, wb, bb)
    x_out[...] = x
    b_out[...] = b
    c_out[...] = conv_silu(pc, rc, wc, bc)
    run = run_ref[0]
    scale = jnp.exp(run[-1:, :] - run) * step_ref[0]
    parts = []
    for pair in range(GROUP_HEADS // 2):
        columns = x[:, pair * 2 * P_SIZE : (pair + 1) * 2 * P_SIZE].astype(jnp.float32)
        parts.append((columns * spread(scale, pair)).astype(jnp.bfloat16))
    weighted = jnp.concatenate(parts, 1)
    state = lax.dot_general(
        b, weighted, (((0,), (0,)), ((), ())), preferred_element_type=jnp.float32
    ).astype(jnp.bfloat16)
    pieces, _, width = state_out.shape
    for piece in range(pieces):
        state_out[piece] = state[:, piece * width : (piece + 1) * width]


def within_kernel(x_ref, b_ref, c_ref, run_ref, run_row_ref, step_row_ref, skip_ref, out_ref):
    rows = x_ref.shape[0]
    scores = lax.dot_general(
        c_ref[...], b_ref[...], (((1,), (1,)), ((), ())), preferred_element_type=jnp.float32
    )
    token = lax.broadcasted_iota(jnp.int32, (rows, rows), 0)
    source = lax.broadcasted_iota(jnp.int32, (rows, rows), 1)
    scores = jnp.where(token >= source, scores, 0.0)
    run = run_ref[0]
    lane = lax.broadcasted_iota(jnp.int32, (rows, 2 * P_SIZE), 1)
    for pair in range(GROUP_HEADS // 2):
        columns = slice(pair * 2 * P_SIZE, (pair + 1) * 2 * P_SIZE)
        x = x_ref[:, columns]
        found = []
        for head in (2 * pair, 2 * pair + 1):
            gap = run[:, head : head + 1] - run_row_ref[head : head + 1, :]
            mix = scores * jnp.exp(jnp.minimum(gap, 0.0)) * step_row_ref[head : head + 1, :]
            found.append(jnp.dot(mix.astype(jnp.bfloat16), x, preferred_element_type=jnp.float32))
        out_ref[:, columns] = (
            jnp.where(lane < P_SIZE, found[0], found[1]) + skip_ref[:, columns] * x.astype(jnp.float32)
        )


def total_kernel(state_ref, gain_ref, total_ref):
    total = state_ref[0].astype(jnp.float32)
    for piece in range(1, state_ref.shape[0]):
        total = gain_ref[piece : piece + 1, :] * total + state_ref[piece].astype(jnp.float32)
    total_ref[...] = total


def entering_kernel(state_ref, gain_ref, totals_ref, coef_ref, out_ref):
    now = coef_ref[0:1, :] * totals_ref[0]
    for section in range(1, totals_ref.shape[0]):
        now = now + coef_ref[section : section + 1, :] * totals_ref[section]
    for piece in range(state_ref.shape[0]):
        out_ref[piece] = now.astype(jnp.bfloat16)
        now = gain_ref[piece : piece + 1, :] * now + state_ref[piece].astype(jnp.float32)


def finish_kernel(within_ref, c_ref, run_ref, enter_ref, out_ref):
    pieces = enter_ref.shape[0]
    enter = jnp.concatenate([enter_ref[piece] for piece in range(pieces)], 1) if pieces > 1 else enter_ref[0]
    carried = jnp.dot(c_ref[...], enter, preferred_element_type=jnp.float32)
    gain = jnp.exp(run_ref[0])
    for pair in range(GROUP_HEADS // 2):
        columns = slice(pair * 2 * P_SIZE, (pair + 1) * 2 * P_SIZE)
        out_ref[:, columns] = (
            within_ref[:, columns] + spread(gain, pair) * carried[:, columns]
        ).astype(jnp.bfloat16)


def params():
    return pltpu.CompilerParams(vmem_limit_bytes=VMEM_LIMIT)


def per_device(projected, conv_weight, conv_bias, step_size, log_decay, skip_gain):
    sections = lax.axis_size("sec")
    targets = lax.axis_size("cp")
    section = lax.axis_index("sec")
    position = lax.axis_index("cp")
    rows = projected.shape[0]
    width = WIDTH_X // targets
    pieces = GROUP_COLS // width
    heads_here = HEAD_COUNT // targets
    rim = passed_along(projected[rows - RIM :], ("sec", "cp"), 1)
    lower = jnp.tril(jnp.ones((rows, rows), jnp.bfloat16))
    running = jnp.dot(lower, log_decay, preferred_element_type=jnp.float32)
    run_row = running.T
    run_cols = running.reshape(rows, G, GROUP_HEADS).transpose(1, 0, 2)
    steps_f = step_size.astype(jnp.float32)
    step_row = steps_f.T
    step_cols = steps_f.reshape(rows, G, GROUP_HEADS).transpose(1, 0, 2)
    skip_cols = jnp.repeat(skip_gain, P_SIZE)[None]
    bias = conv_bias[None]
    ends = lax.all_gather(running[rows - 1 :], ("sec", "cp"), axis=0, tiled=True)
    ends = ends.reshape(sections, targets, HEAD_COUNT)
    ends = lax.dynamic_slice_in_dim(ends, position * heads_here, heads_here, 2)
    mine = lax.dynamic_slice_in_dim(ends, section, 1, 0)[0]
    gain = jnp.repeat(jnp.exp(mine), P_SIZE, axis=1)
    through = jnp.cumsum(jnp.sum(ends, 1), axis=0)
    before = jnp.where(section > 0, lax.dynamic_slice_in_dim(through, jnp.maximum(section - 1, 0), 1, 0), 0.0)
    earlier = lax.broadcasted_iota(jnp.int32, through.shape, 0) < section
    coef = jnp.where(earlier, jnp.exp(jnp.minimum(before - through, 0.0)), 0.0)
    coef = jnp.repeat(coef, P_SIZE, axis=1)

    def spec(height, cols, first):
        return pl.BlockSpec((height, cols), lambda g: (0, first + g))

    def three(height):
        return [spec(height, GROUP_COLS, 0), spec(height, N, WIDTH_X // N), spec(height, N, WIDTH_X // N + G)]

    group_cols = pl.BlockSpec((1, rows, GROUP_HEADS), lambda g: (g, 0, 0))
    group_rows = pl.BlockSpec((GROUP_HEADS, rows), lambda g: (g, 0))
    piece_spec = pl.BlockSpec((pieces, N, width), lambda g: (g, 0, 0))
    x, b, c, state = pl.pallas_call(
        conv_state_kernel,
        grid=(G,),
        in_specs=three(rows) + three(RIM) + three(KERNEL) + three(1) + [group_cols, group_cols],
        out_specs=[spec(rows, GROUP_COLS, 0), spec(rows, N, 0), spec(rows, N, 0), piece_spec],
        out_shape=[
            jax.ShapeDtypeStruct((rows, WIDTH_X), jnp.bfloat16),
            jax.ShapeDtypeStruct((rows, G * N), jnp.bfloat16),
            jax.ShapeDtypeStruct((rows, G * N), jnp.bfloat16),
            jax.ShapeDtypeStruct((targets, N, width), jnp.bfloat16),
        ],
        compiler_params=params(),
        name="conv_state",
    )(*([projected] * 3), *([rim] * 3), *([conv_weight] * 3), *([bias] * 3), run_cols, step_cols)
    state = lax.all_to_all(state, "cp", split_axis=0, concat_axis=0, tiled=True)
    within = pl.pallas_call(
        within_kernel,
        grid=(G,),
        in_specs=[spec(rows, GROUP_COLS, 0), spec(rows, N, 0), spec(rows, N, 0), group_cols, group_rows, group_rows, spec(1, GROUP_COLS, 0)],
        out_specs=spec(rows, GROUP_COLS, 0),
        out_shape=jax.ShapeDtypeStruct((rows, WIDTH_X), jnp.float32),
        compiler_params=params(),
        cost_estimate=pl.CostEstimate(flops=2 * 2 * HEAD_COUNT * rows * rows * N, bytes_accessed=8 * 1024 * 1024, transcendentals=HEAD_COUNT * rows * rows),
        name="within",
    )(x, b, c, run_cols, run_row, step_row, skip_cols)
    total = pl.pallas_call(
        total_kernel,
        out_shape=jax.ShapeDtypeStruct((N, width), jnp.float32),
        compiler_params=params(),
        name="section_total",
    )(state, gain)
    totals = lax.all_gather(total, "sec", axis=0)
    entering = pl.pallas_call(
        entering_kernel,
        out_shape=jax.ShapeDtypeStruct((targets, N, width), jnp.bfloat16),
        compiler_params=params(),
        name="entering",
    )(state, gain, totals, coef)
    entering = lax.all_to_all(entering, "cp", split_axis=0, concat_axis=0, tiled=True)
    return pl.pallas_call(
        finish_kernel,
        grid=(G,),
        in_specs=[spec(rows, GROUP_COLS, 0), spec(rows, N, 0), group_cols, piece_spec],
        out_specs=spec(rows, GROUP_COLS, 0),
        out_shape=jax.ShapeDtypeStruct((rows, WIDTH_X), jnp.bfloat16),
        compiler_params=params(),
        name="finish",
    )(within, c, run_cols, entering)


def solution(mesh):
    in_specs = (
        P(("sec", "cp"), None),
        P(),
        P(),
        P(("sec", "cp"), None),
        P(("sec", "cp"), None),
        P(),
    )
    out_specs = P(("sec", "cp"), None)
    return jax.shard_map(
        per_device, mesh=mesh, in_specs=in_specs, out_specs=out_specs, check_vma=False
    )
```

```python
import functools
import jax
import jax.numpy as jnp
from jax import lax
from jax.experimental import pallas as pl
from jax.experimental.pallas import tpu as pltpu
from jax.sharding import PartitionSpec as P

HEAD_COUNT = 128
P_SIZE = 64
N = 128
G = 8
KERNEL = 4
GROUP_HEADS = HEAD_COUNT // G
GROUP_COLS = GROUP_HEADS * P_SIZE
WIDTH_X = HEAD_COUNT * P_SIZE
RIM = 8
CHUNKS = 4
VMEM_LIMIT = 48 * 1024 * 1024


def passed_along(value, axis, steps):
    count = lax.axis_size(axis)
    return lax.ppermute(value, axis, [(source, source + steps) for source in range(count - steps)])


def conv_silu(block_ref, rim_ref, weight_ref, bias_ref):
    now = block_ref[...].astype(jnp.float32)
    rim = rim_ref[...].astype(jnp.float32)
    row = lax.broadcasted_iota(jnp.int32, rim.shape, 0)
    total = bias_ref[...] + weight_ref[KERNEL - 1 : KERNEL, :] * now
    for back in range(1, KERNEL):
        moved = pltpu.roll(now, back, 0)
        top = jnp.where(row < back, pltpu.roll(rim, back, 0), moved[:RIM])
        moved = jnp.concatenate([top, moved[RIM:]], 0)
        total = total + weight_ref[KERNEL - 1 - back : KERNEL - back, :] * moved
    return (total / (1.0 + jnp.exp(-total))).astype(jnp.bfloat16)


def spread(columns, pair):
    rows = columns.shape[0]
    lane = lax.broadcasted_iota(jnp.int32, (rows, 2 * P_SIZE), 1)
    return jnp.where(lane < P_SIZE, columns[:, 2 * pair : 2 * pair + 1], columns[:, 2 * pair + 1 : 2 * pair + 2])


def conv_state_kernel(
    px, pb, pc, rx, rb, rc, wx, wb, wc, bx, bb, bc, run_ref, step_ref,
    x_out, b_out, c_out, state_out,
):
    x = conv_silu(px, rx, wx, bx)
    b = conv_silu(pb, rb, wb, bb)
    x_out[...] = x
    b_out[...] = b
    c_out[...] = conv_silu(pc, rc, wc, bc)
    run = run_ref[0]
    scale = jnp.exp(run[-1:, :] - run) * step_ref[0]
    parts = []
    for pair in range(GROUP_HEADS // 2):
        columns = x[:, pair * 2 * P_SIZE : (pair + 1) * 2 * P_SIZE].astype(jnp.float32)
        parts.append((columns * spread(scale, pair)).astype(jnp.bfloat16))
    weighted = jnp.concatenate(parts, 1)
    state = lax.dot_general(
        b, weighted, (((0,), (0,)), ((), ())), preferred_element_type=jnp.float32
    ).astype(jnp.bfloat16)
    _, chunks, places, _, width = state_out.shape
    for place in range(places):
        for chunk in range(chunks):
            begin = (place * chunks + chunk) * width
            state_out[0, chunk, place] = state[:, begin : begin + width]


def within_kernel(x_ref, b_ref, c_ref, run_ref, run_row_ref, step_row_ref, skip_ref, out_ref):
    rows = x_ref.shape[0]
    scores = lax.dot_general(
        c_ref[...], b_ref[...], (((1,), (1,)), ((), ())), preferred_element_type=jnp.float32
    )
    token = lax.broadcasted_iota(jnp.int32, (rows, rows), 0)
    source = lax.broadcasted_iota(jnp.int32, (rows, rows), 1)
    scores = jnp.where(token >= source, scores, 0.0)
    run = run_ref[0]
    lane = lax.broadcasted_iota(jnp.int32, (rows, 2 * P_SIZE), 1)
    for pair in range(GROUP_HEADS // 2):
        columns = slice(pair * 2 * P_SIZE, (pair + 1) * 2 * P_SIZE)
        x = x_ref[:, columns]
        found = []
        for head in (2 * pair, 2 * pair + 1):
            gap = run[:, head : head + 1] - run_row_ref[head : head + 1, :]
            mix = scores * jnp.exp(jnp.minimum(gap, 0.0)) * step_row_ref[head : head + 1, :]
            found.append(jnp.dot(mix.astype(jnp.bfloat16), x, preferred_element_type=jnp.float32))
        out_ref[:, columns] = (
            jnp.where(lane < P_SIZE, found[0], found[1]) + skip_ref[:, columns] * x.astype(jnp.float32)
        )


def scan_kernel(
    state_ref, gain_ref, out_ref,
    from_pair, block_send, block_recv, total_send, total_recv, enter_send, enter_recv, back_send,
    pair_gain, block_gain, block_gains, section_gain, section_gains,
    pair_sems, block_sems, total_sems, enter_sems, back_sems, pair_gain_sems, block_gain_sems, section_gain_sems,
):
    sections = lax.axis_size("sec")
    section, position = lax.axis_index("sec"), lax.axis_index("cp")
    place, side = position // 2, position % 2
    _, chunks, places, rows, width = state_ref.shape
    first = side == 0
    partner = (section, place * 2 + (1 - side))
    near = [lax.rem(place + step, places) for step in range(1, places)]
    line = [(section, other * 2 + side) for other in near]
    above = [(lax.rem(section + step, sections), position) for step in range(1, sections)]

    def remote(source, target, sems, at, device):
        return pltpu.make_async_remote_copy(
            src_ref=source,
            dst_ref=target,
            send_sem=sems.at[(0, *at)],
            recv_sem=sems.at[(1, *at)],
            device_id=device,
            device_id_type=pl.DeviceIdType.MESH,
        )

    barrier = pltpu.get_barrier_semaphore()
    for device in [partner, *line, *above]:
        pl.semaphore_signal(barrier, inc=1, device_id=device, device_id_type=pl.DeviceIdType.MESH)
    pl.semaphore_wait(barrier, len(line) + len(above) + 1)

    started = []

    def begin(copy):
        copy.start()
        started.append(copy)
        return copy

    pair_gain_copy = begin(remote(gain_ref.at[1 - side], pair_gain, pair_gain_sems, (0,), partner))
    pair_copies = [
        begin(remote(state_ref.at[1 - side, chunk], from_pair.at[chunk], pair_sems, (chunk,), partner))
        for chunk in range(chunks)
    ]
    pair_gain_copy.wait_recv()
    block_gain[...] = gain_ref[side] * pair_gain[...]
    block_gains[place] = block_gain[place]
    block_gain_copies = [
        begin(remote(block_gain.at[other], block_gains.at[place], block_gain_sems, (step,), device))
        for step, (other, device) in enumerate(zip(near, line))
    ]
    block_copies, total_copies, enter_copies, back_copies = {}, {}, {}, {}
    section_gain_copies = []

    def pair_order(chunk, slot):
        own = state_ref[side, chunk, slot].astype(jnp.float32)
        other = from_pair[chunk, slot].astype(jnp.float32)
        return own, other

    def stage_block(chunk):
        pair_copies[chunk].wait_recv()
        for slot in range(places):
            own, other = pair_order(chunk, slot)
            early, late = jnp.where(first, own, other), jnp.where(first, other, own)
            late_gain = jnp.where(first, pair_gain[slot, chunk], gain_ref[side, slot, chunk])
            block_send[chunk, slot] = (late_gain * early + late).astype(jnp.bfloat16)
        block_recv[chunk, place] = block_send[chunk, place]
        block_copies[chunk] = [
            begin(remote(block_send.at[chunk, other], block_recv.at[chunk, place], block_sems, (chunk, step), device))
            for step, (other, device) in enumerate(zip(near, line))
        ]

    def stage_total(chunk):
        if chunk == 0:
            for copy in block_gain_copies:
                copy.wait_recv()
            product = block_gains[0]
            for slot in range(1, places):
                product = product * block_gains[slot]
            section_gain[...] = product
            section_gains[section] = product
            for step, device in enumerate(above):
                section_gain_copies.append(
                    begin(remote(section_gain, section_gains.at[section], section_gain_sems, (step,), device))
                )
        for copy in block_copies[chunk]:
            copy.wait_recv()
        total = block_recv[chunk, 0].astype(jnp.float32)
        for slot in range(1, places):
            total = block_gains[slot, chunk] * total + block_recv[chunk, slot].astype(jnp.float32)
        total = total.astype(jnp.bfloat16)
        total_send[chunk] = total
        total_recv[chunk, section] = total
        total_copies[chunk] = [
            begin(remote(total_send.at[chunk], total_recv.at[chunk, section], total_sems, (chunk, step), device))
            for step, device in enumerate(above)
        ]

    def stage_enter(chunk):
        if chunk == 0:
            for copy in section_gain_copies:
                copy.wait_recv()
        for copy in total_copies[chunk]:
            copy.wait_recv()
        now = jnp.zeros((rows, width), jnp.float32)
        for other in range(sections - 1):
            later = section_gains[other, chunk] * now + total_recv[chunk, other].astype(jnp.float32)
            now = jnp.where(other < section, later, now)
        for slot in range(places):
            enter_send[chunk, slot] = now.astype(jnp.bfloat16)
            if slot < places - 1:
                now = block_gains[slot, chunk] * now + block_recv[chunk, slot].astype(jnp.float32)
        enter_recv[chunk, place] = enter_send[chunk, place]
        enter_copies[chunk] = [
            begin(remote(enter_send.at[chunk, other], enter_recv.at[chunk, place], enter_sems, (chunk, step), device))
            for step, (other, device) in enumerate(zip(near, line))
        ]

    def stage_back(chunk):
        for copy in enter_copies[chunk]:
            copy.wait_recv()
        for slot in range(places):
            own, other = pair_order(chunk, slot)
            early = jnp.where(first, own, other)
            early_gain = jnp.where(first, gain_ref[side, slot, chunk], pair_gain[slot, chunk])
            into_block = enter_recv[chunk, slot]
            into_late = (early_gain * into_block.astype(jnp.float32) + early).astype(jnp.bfloat16)
            out_ref[side, chunk, slot] = jnp.where(first, into_block, into_late)
            back_send[chunk, slot] = jnp.where(first, into_late, into_block)
        back_copies[chunk] = begin(
            remote(back_send.at[chunk], out_ref.at[side, chunk], back_sems, (chunk,), partner)
        )

    for turn in range(chunks + 3):
        for stage, lag in ((stage_block, 0), (stage_total, 1), (stage_enter, 2), (stage_back, 3)):
            if 0 <= turn - lag < chunks:
                stage(turn - lag)
    for chunk in range(chunks):
        back_copies[chunk].wait_recv()
    for copy in started:
        copy.wait_send()


def finish_kernel(within_ref, c_ref, run_ref, enter_ref, out_ref):
    _, chunks, places, _, _ = enter_ref.shape
    enter = jnp.concatenate(
        [enter_ref[0, chunk, place] for place in range(places) for chunk in range(chunks)], 1
    )
    carried = jnp.dot(c_ref[...], enter, preferred_element_type=jnp.float32)
    gain = jnp.exp(run_ref[0])
    for pair in range(GROUP_HEADS // 2):
        columns = slice(pair * 2 * P_SIZE, (pair + 1) * 2 * P_SIZE)
        out_ref[:, columns] = (
            within_ref[:, columns] + spread(gain, pair) * carried[:, columns]
        ).astype(jnp.bfloat16)


def params():
    return pltpu.CompilerParams(vmem_limit_bytes=VMEM_LIMIT)


def per_device(projected, conv_weight, conv_bias, step_size, log_decay, skip_gain):
    sections = lax.axis_size("sec")
    places = lax.axis_size("cp") // 2
    rows = projected.shape[0]
    place_cols = WIDTH_X // 2 // places
    chunks = max(1, min(CHUNKS, place_cols // 128))
    width = place_cols // chunks
    group_places = GROUP_COLS // place_cols
    half_groups = G // 2
    rim = passed_along(projected[rows - RIM :], ("sec", "cp"), 1)
    lower = jnp.tril(jnp.ones((rows, rows), jnp.bfloat16))
    running = jnp.dot(lower, log_decay, preferred_element_type=jnp.float32)
    run_row = running.T
    run_cols = running.reshape(rows, G, GROUP_HEADS).transpose(1, 0, 2)
    steps_f = step_size.astype(jnp.float32)
    step_row = steps_f.T
    step_cols = steps_f.reshape(rows, G, GROUP_HEADS).transpose(1, 0, 2)
    skip_cols = jnp.repeat(skip_gain, P_SIZE)[None]
    bias = conv_bias[None]
    gain = jnp.repeat(jnp.exp(running[rows - 1]), P_SIZE).reshape(2, places, chunks, 1, width)

    def spec(height, cols, first):
        return pl.BlockSpec((height, cols), lambda g: (0, first + g))

    def three(height):
        return [spec(height, GROUP_COLS, 0), spec(height, N, WIDTH_X // N), spec(height, N, WIDTH_X // N + G)]

    group_cols = pl.BlockSpec((1, rows, GROUP_HEADS), lambda g: (g, 0, 0))
    group_rows = pl.BlockSpec((GROUP_HEADS, rows), lambda g: (g, 0))
    piece_spec = pl.BlockSpec(
        (1, chunks, group_places, N, width), lambda g: (g // half_groups, 0, g % half_groups, 0, 0)
    )
    state_shape = jax.ShapeDtypeStruct((2, chunks, places, N, width), jnp.bfloat16)
    x, b, c, state = pl.pallas_call(
        conv_state_kernel,
        grid=(G,),
        in_specs=three(rows) + three(RIM) + three(KERNEL) + three(1) + [group_cols, group_cols],
        out_specs=[spec(rows, GROUP_COLS, 0), spec(rows, N, 0), spec(rows, N, 0), piece_spec],
        out_shape=[
            jax.ShapeDtypeStruct((rows, WIDTH_X), jnp.bfloat16),
            jax.ShapeDtypeStruct((rows, G * N), jnp.bfloat16),
            jax.ShapeDtypeStruct((rows, G * N), jnp.bfloat16),
            state_shape,
        ],
        compiler_params=params(),
        name="conv_state",
    )(*([projected] * 3), *([rim] * 3), *([conv_weight] * 3), *([bias] * 3), run_cols, step_cols)
    within = pl.pallas_call(
        within_kernel,
        grid=(G,),
        in_specs=[spec(rows, GROUP_COLS, 0), spec(rows, N, 0), spec(rows, N, 0), group_cols, group_rows, group_rows, spec(1, GROUP_COLS, 0)],
        out_specs=spec(rows, GROUP_COLS, 0),
        out_shape=jax.ShapeDtypeStruct((rows, WIDTH_X), jnp.float32),
        compiler_params=params(),
        cost_estimate=pl.CostEstimate(flops=2 * 2 * HEAD_COUNT * rows * rows * N, bytes_accessed=8 * 1024 * 1024, transcendentals=HEAD_COUNT * rows * rows),
        name="within",
    )(x, b, c, run_cols, run_row, step_row, skip_cols)
    whole = pl.BlockSpec(memory_space=pltpu.VMEM)

    def held(*shape):
        return pltpu.VMEM((*shape, N, width), jnp.bfloat16)

    def gains(*shape):
        return pltpu.VMEM((*shape, chunks, 1, width), jnp.float32)

    def sems(*shape):
        return pltpu.SemaphoreType.DMA((2, *shape))

    entering = pl.pallas_call(
        scan_kernel,
        in_specs=[whole, whole],
        out_specs=whole,
        out_shape=state_shape,
        scratch_shapes=[
            held(chunks, places),
            held(chunks, places),
            held(chunks, places),
            held(chunks),
            held(chunks, sections),
            held(chunks, places),
            held(chunks, places),
            held(chunks, places),
            gains(places),
            gains(places),
            gains(places),
            gains(),
            gains(sections),
            sems(chunks),
            sems(chunks, places - 1),
            sems(chunks, sections - 1),
            sems(chunks, places - 1),
            sems(chunks),
            sems(1),
            sems(places - 1),
            sems(sections - 1),
        ],
        compiler_params=pltpu.CompilerParams(
            vmem_limit_bytes=VMEM_LIMIT, collective_id=0, has_side_effects=True
        ),
        name="state_scan",
    )(state, gain)
    return pl.pallas_call(
        finish_kernel,
        grid=(G,),
        in_specs=[spec(rows, GROUP_COLS, 0), spec(rows, N, 0), group_cols, piece_spec],
        out_specs=spec(rows, GROUP_COLS, 0),
        out_shape=jax.ShapeDtypeStruct((rows, WIDTH_X), jnp.bfloat16),
        compiler_params=params(),
        name="finish",
    )(within, c, run_cols, entering)


def solution(mesh):
    in_specs = (
        P(("sec", "cp"), None),
        P(),
        P(),
        P(("sec", "cp"), None),
        P(("sec", "cp"), None),
        P(),
    )
    out_specs = P(("sec", "cp"), None)
    return jax.shard_map(
        per_device, mesh=mesh, in_specs=in_specs, out_specs=out_specs, check_vma=False
    )
```

```python
import functools
import jax
import jax.numpy as jnp
from jax import lax
from jax.experimental import pallas as pl
from jax.experimental.pallas import tpu as pltpu
from jax.sharding import PartitionSpec as P

HEAD_COUNT = 128
P_SIZE = 64
N = 128
G = 8
KERNEL = 4
GROUP_HEADS = HEAD_COUNT // G
GROUP_COLS = GROUP_HEADS * P_SIZE
WIDTH_X = HEAD_COUNT * P_SIZE
RIM = 8
VMEM_LIMIT = 48 * 1024 * 1024


def passed_along(value, axis, steps):
    count = lax.axis_size(axis)
    return lax.ppermute(value, axis, [(source, source + steps) for source in range(count - steps)])


def conv_silu(block_ref, rim_ref, weight_ref, bias_ref):
    now = block_ref[...].astype(jnp.float32)
    rim = rim_ref[...].astype(jnp.float32)
    row = lax.broadcasted_iota(jnp.int32, rim.shape, 0)
    total = bias_ref[...] + weight_ref[KERNEL - 1 : KERNEL, :] * now
    for back in range(1, KERNEL):
        moved = pltpu.roll(now, back, 0)
        top = jnp.where(row < back, pltpu.roll(rim, back, 0), moved[:RIM])
        moved = jnp.concatenate([top, moved[RIM:]], 0)
        total = total + weight_ref[KERNEL - 1 - back : KERNEL - back, :] * moved
    return (total / (1.0 + jnp.exp(-total))).astype(jnp.bfloat16)


def spread(columns, pair):
    rows = columns.shape[0]
    lane = lax.broadcasted_iota(jnp.int32, (rows, 2 * P_SIZE), 1)
    return jnp.where(lane < P_SIZE, columns[:, 2 * pair : 2 * pair + 1], columns[:, 2 * pair + 1 : 2 * pair + 2])


def conv_state_kernel(
    px, pb, pc, rx, rb, rc, wx, wb, wc, bx, bb, bc, run_ref, step_ref,
    x_out, b_out, c_out, state_out,
):
    x = conv_silu(px, rx, wx, bx)
    b = conv_silu(pb, rb, wb, bb)
    x_out[...] = x
    b_out[...] = b
    c_out[...] = conv_silu(pc, rc, wc, bc)
    run = run_ref[0]
    scale = jnp.exp(run[-1:, :] - run) * step_ref[0]
    parts = []
    for pair in range(GROUP_HEADS // 2):
        columns = x[:, pair * 2 * P_SIZE : (pair + 1) * 2 * P_SIZE].astype(jnp.float32)
        parts.append((columns * spread(scale, pair)).astype(jnp.bfloat16))
    weighted = jnp.concatenate(parts, 1)
    state = lax.dot_general(
        b, weighted, (((0,), (0,)), ((), ())), preferred_element_type=jnp.float32
    ).astype(jnp.bfloat16)
    _, chunks, places, _, width = state_out.shape
    for place in range(places):
        for chunk in range(chunks):
            begin = (place * chunks + chunk) * width
            state_out[0, chunk, place] = state[:, begin : begin + width]


def scan_kernel(
    state_ref, gain_ref, x_ref, b_ref, c_ref, run_ref, run_row_ref, step_row_ref, skip_ref, out_ref,
    enter_ref, run_pair, scores_ref, within_ref, from_pair, block_send, block_recv, total_send, total_recv, enter_send, enter_recv, back_send,
    pair_gain, block_gain, block_gains, section_gain, section_gains,
    pair_sems, block_sems, total_sems, enter_sems, back_sems, pair_gain_sems, block_gain_sems, section_gain_sems,
):
    sections = lax.axis_size("sec")
    section, position = lax.axis_index("sec"), lax.axis_index("cp")
    place, side = position // 2, position % 2
    _, chunks, places, rows, width = state_ref.shape
    tokens = x_ref.shape[0]
    lane = lax.broadcasted_iota(jnp.int32, (tokens, width), 1)
    first = side == 0
    partner = (section, place * 2 + (1 - side))
    near = [lax.rem(place + step, places) for step in range(1, places)]
    line = [(section, other * 2 + side) for other in near]
    above = [(lax.rem(section + step, sections), position) for step in range(1, sections)]

    def remote(source, target, sems, at, device):
        return pltpu.make_async_remote_copy(
            src_ref=source,
            dst_ref=target,
            send_sem=sems.at[(0, *at)],
            recv_sem=sems.at[(1, *at)],
            device_id=device,
            device_id_type=pl.DeviceIdType.MESH,
        )

    barrier = pltpu.get_barrier_semaphore()
    for device in [partner, *line, *above]:
        pl.semaphore_signal(barrier, inc=1, device_id=device, device_id_type=pl.DeviceIdType.MESH)
    pl.semaphore_wait(barrier, len(line) + len(above) + 1)

    started = []

    def begin(copy):
        copy.start()
        started.append(copy)
        return copy

    pair_gain_copy = begin(remote(gain_ref.at[1 - side], pair_gain, pair_gain_sems, (0,), partner))
    pair_copies = [
        begin(remote(state_ref.at[1 - side, chunk], from_pair.at[chunk], pair_sems, (chunk,), partner))
        for chunk in range(chunks)
    ]

    for pair in range(HEAD_COUNT // 2):
        run_pair[pair] = run_ref[:, 2 * pair : 2 * pair + 2]
    token = lax.broadcasted_iota(jnp.int32, (tokens, tokens), 0)
    causal = token >= lax.broadcasted_iota(jnp.int32, (tokens, tokens), 1)

    def group_scores(group, carry):
        columns = pl.ds(pl.multiple_of(group * N, N), N)
        scores = lax.dot_general(
            c_ref[:, columns], b_ref[:, columns], (((1,), (1,)), ((), ())), preferred_element_type=jnp.float32
        )
        scores_ref[group] = jnp.where(causal, scores, 0.0)
        return carry

    lax.fori_loop(0, G, group_scores, 0)

    def stage_within(chunk):
        def one_place(slot, carry):
            for half in range(2):
                pair = (half * places + slot) * chunks + chunk
                columns = pl.ds(pl.multiple_of(pair * width, width), width)
                scores = scores_ref[lax.div(pair, GROUP_HEADS // 2)]
                x = x_ref[:, columns]
                run = run_pair[pair]
                run_row = run_row_ref[pair]
                step_row = step_row_ref[pair]
                found = []
                for head in range(2):
                    gap = run[:, head : head + 1] - run_row[head : head + 1, :]
                    mix = scores * jnp.exp(jnp.minimum(gap, 0.0)) * step_row[head : head + 1, :]
                    found.append(jnp.dot(mix.astype(jnp.bfloat16), x, preferred_element_type=jnp.float32))
                within_ref[pair] = (
                    jnp.where(lane < P_SIZE, found[0], found[1]) + skip_ref[pair] * x.astype(jnp.float32)
                )
            return carry

        lax.fori_loop(0, places, one_place, 0)

    def stage_finish(chunk):
        back_copies[chunk].wait_recv()

        def one_place(slot, carry):
            for half in range(2):
                pair = (half * places + slot) * chunks + chunk
                group = lax.div(pair, GROUP_HEADS // 2)
                carried = jnp.dot(
                    c_ref[:, pl.ds(pl.multiple_of(group * N, N), N)],
                    enter_ref[half, chunk, slot],
                    preferred_element_type=jnp.float32,
                )
                gain = jnp.exp(run_pair[pair])
                out_ref[:, pl.ds(pl.multiple_of(pair * width, width), width)] = (
                    within_ref[pair] + spread(gain, 0) * carried
                ).astype(jnp.bfloat16)
            return carry

        lax.fori_loop(0, places, one_place, 0)

    pair_gain_copy.wait_recv()
    block_gain[...] = gain_ref[side] * pair_gain[...]
    block_gains[place] = block_gain[place]
    block_gain_copies = [
        begin(remote(block_gain.at[other], block_gains.at[place], block_gain_sems, (step,), device))
        for step, (other, device) in enumerate(zip(near, line))
    ]
    block_copies, total_copies, enter_copies, back_copies = {}, {}, {}, {}
    section_gain_copies = []

    def pair_order(chunk, slot):
        own = state_ref[side, chunk, slot].astype(jnp.float32)
        other = from_pair[chunk, slot].astype(jnp.float32)
        return own, other

    def stage_block(chunk):
        pair_copies[chunk].wait_recv()
        for slot in range(places):
            own, other = pair_order(chunk, slot)
            early, late = jnp.where(first, own, other), jnp.where(first, other, own)
            late_gain = jnp.where(first, pair_gain[slot, chunk], gain_ref[side, slot, chunk])
            block_send[chunk, slot] = (late_gain * early + late).astype(jnp.bfloat16)
        block_recv[chunk, place] = block_send[chunk, place]
        block_copies[chunk] = [
            begin(remote(block_send.at[chunk, other], block_recv.at[chunk, place], block_sems, (chunk, step), device))
            for step, (other, device) in enumerate(zip(near, line))
        ]

    def stage_total(chunk):
        if chunk == 0:
            for copy in block_gain_copies:
                copy.wait_recv()
            product = block_gains[0]
            for slot in range(1, places):
                product = product * block_gains[slot]
            section_gain[...] = product
            section_gains[section] = product
            for step, device in enumerate(above):
                section_gain_copies.append(
                    begin(remote(section_gain, section_gains.at[section], section_gain_sems, (step,), device))
                )
        for copy in block_copies[chunk]:
            copy.wait_recv()
        total = block_recv[chunk, 0].astype(jnp.float32)
        for slot in range(1, places):
            total = block_gains[slot, chunk] * total + block_recv[chunk, slot].astype(jnp.float32)
        total = total.astype(jnp.bfloat16)
        total_send[chunk] = total
        total_recv[chunk, section] = total
        total_copies[chunk] = [
            begin(remote(total_send.at[chunk], total_recv.at[chunk, section], total_sems, (chunk, step), device))
            for step, device in enumerate(above)
        ]

    def stage_enter(chunk):
        if chunk == 0:
            for copy in section_gain_copies:
                copy.wait_recv()
        for copy in total_copies[chunk]:
            copy.wait_recv()
        now = jnp.zeros((rows, width), jnp.float32)
        for other in range(sections - 1):
            later = section_gains[other, chunk] * now + total_recv[chunk, other].astype(jnp.float32)
            now = jnp.where(other < section, later, now)
        for slot in range(places):
            enter_send[chunk, slot] = now.astype(jnp.bfloat16)
            if slot < places - 1:
                now = block_gains[slot, chunk] * now + block_recv[chunk, slot].astype(jnp.float32)
        enter_recv[chunk, place] = enter_send[chunk, place]
        enter_copies[chunk] = [
            begin(remote(enter_send.at[chunk, other], enter_recv.at[chunk, place], enter_sems, (chunk, step), device))
            for step, (other, device) in enumerate(zip(near, line))
        ]

    def stage_back(chunk):
        for copy in enter_copies[chunk]:
            copy.wait_recv()
        for slot in range(places):
            own, other = pair_order(chunk, slot)
            early = jnp.where(first, own, other)
            early_gain = jnp.where(first, gain_ref[side, slot, chunk], pair_gain[slot, chunk])
            into_block = enter_recv[chunk, slot]
            into_late = (early_gain * into_block.astype(jnp.float32) + early).astype(jnp.bfloat16)
            enter_ref[side, chunk, slot] = jnp.where(first, into_block, into_late)
            back_send[chunk, slot] = jnp.where(first, into_late, into_block)
        back_copies[chunk] = begin(
            remote(back_send.at[chunk], enter_ref.at[side, chunk], back_sems, (chunk,), partner)
        )

    plan = ((stage_block, 0), (stage_within, 0), (stage_total, 1), (stage_enter, 2), (stage_back, 3), (stage_finish, 4))
    for turn in range(chunks + 4):
        for stage, lag in plan:
            if 0 <= turn - lag < chunks:
                stage(turn - lag)
    for copy in started:
        copy.wait_send()


def params():
    return pltpu.CompilerParams(vmem_limit_bytes=VMEM_LIMIT)


def per_device(projected, conv_weight, conv_bias, step_size, log_decay, skip_gain):
    sections = lax.axis_size("sec")
    places = lax.axis_size("cp") // 2
    rows = projected.shape[0]
    place_cols = WIDTH_X // 2 // places
    width = 2 * P_SIZE
    chunks = place_cols // width
    pairs = HEAD_COUNT // 2
    group_places = GROUP_COLS // place_cols
    half_groups = G // 2
    rim = passed_along(projected[rows - RIM :], ("sec", "cp"), 1)
    lower = jnp.tril(jnp.ones((rows, rows), jnp.bfloat16))
    running = jnp.dot(lower, log_decay, preferred_element_type=jnp.float32)
    run_row = running.T.reshape(pairs, 2, rows)
    run_cols = running.reshape(rows, G, GROUP_HEADS).transpose(1, 0, 2)
    steps_f = step_size.astype(jnp.float32)
    step_row = steps_f.T.reshape(pairs, 2, rows)
    step_cols = steps_f.reshape(rows, G, GROUP_HEADS).transpose(1, 0, 2)
    skip_cols = jnp.repeat(skip_gain, P_SIZE).reshape(pairs, 1, width)
    bias = conv_bias[None]
    gain = jnp.repeat(jnp.exp(running[rows - 1]), P_SIZE).reshape(2, places, chunks, 1, width)

    def spec(height, cols, first):
        return pl.BlockSpec((height, cols), lambda g: (0, first + g))

    def three(height):
        return [spec(height, GROUP_COLS, 0), spec(height, N, WIDTH_X // N), spec(height, N, WIDTH_X // N + G)]

    group_cols = pl.BlockSpec((1, rows, GROUP_HEADS), lambda g: (g, 0, 0))
    piece_spec = pl.BlockSpec(
        (1, chunks, group_places, N, width), lambda g: (g // half_groups, 0, g % half_groups, 0, 0)
    )
    state_shape = jax.ShapeDtypeStruct((2, chunks, places, N, width), jnp.bfloat16)
    x, b, c, state = pl.pallas_call(
        conv_state_kernel,
        grid=(G,),
        in_specs=three(rows) + three(RIM) + three(KERNEL) + three(1) + [group_cols, group_cols],
        out_specs=[spec(rows, GROUP_COLS, 0), spec(rows, N, 0), spec(rows, N, 0), piece_spec],
        out_shape=[
            jax.ShapeDtypeStruct((rows, WIDTH_X), jnp.bfloat16),
            jax.ShapeDtypeStruct((rows, G * N), jnp.bfloat16),
            jax.ShapeDtypeStruct((rows, G * N), jnp.bfloat16),
            state_shape,
        ],
        compiler_params=params(),
        name="conv_state",
    )(*([projected] * 3), *([rim] * 3), *([conv_weight] * 3), *([bias] * 3), run_cols, step_cols)
    whole = pl.BlockSpec(memory_space=pltpu.VMEM)

    def held(*shape):
        return pltpu.VMEM((*shape, N, width), jnp.bfloat16)

    def gains(*shape):
        return pltpu.VMEM((*shape, chunks, 1, width), jnp.float32)

    def sems(*shape):
        return pltpu.SemaphoreType.DMA((2, *shape))

    return pl.pallas_call(
        scan_kernel,
        in_specs=[whole] * 9,
        out_specs=whole,
        out_shape=jax.ShapeDtypeStruct((rows, WIDTH_X), jnp.bfloat16),
        scratch_shapes=[
            held(2, chunks, places),
            pltpu.VMEM((pairs, rows, 2), jnp.float32),
            pltpu.VMEM((G, rows, rows), jnp.float32),
            pltpu.VMEM((pairs, rows, width), jnp.float32),
            held(chunks, places),
            held(chunks, places),
            held(chunks, places),
            held(chunks),
            held(chunks, sections),
            held(chunks, places),
            held(chunks, places),
            held(chunks, places),
            gains(places),
            gains(places),
            gains(places),
            gains(),
            gains(sections),
            sems(chunks),
            sems(chunks, places - 1),
            sems(chunks, sections - 1),
            sems(chunks, places - 1),
            sems(chunks),
            sems(1),
            sems(places - 1),
            sems(sections - 1),
        ],
        compiler_params=pltpu.CompilerParams(
            vmem_limit_bytes=VMEM_LIMIT, collective_id=0, has_side_effects=True
        ),
        name="state_scan",
    )(state, gain, x, b, c, running, run_row, step_row, skip_cols)


def solution(mesh):
    in_specs = (
        P(("sec", "cp"), None),
        P(),
        P(),
        P(("sec", "cp"), None),
        P(("sec", "cp"), None),
        P(),
    )
    out_specs = P(("sec", "cp"), None)
    return jax.shard_map(
        per_device, mesh=mesh, in_specs=in_specs, out_specs=out_specs, check_vma=False
    )
```

```python
import functools
import jax
import jax.numpy as jnp
from jax import lax
from jax.experimental import pallas as pl
from jax.experimental.pallas import tpu as pltpu
from jax.sharding import PartitionSpec as P

HEAD_COUNT = 128
P_SIZE = 64
N = 128
G = 8
KERNEL = 4
GROUP_HEADS = HEAD_COUNT // G
GROUP_COLS = GROUP_HEADS * P_SIZE
WIDTH_X = HEAD_COUNT * P_SIZE
RIM = 8
IN_FLIGHT = 3
VMEM_LIMIT = 48 * 1024 * 1024


def passed_along(value, axis, steps):
    count = lax.axis_size(axis)
    return lax.ppermute(value, axis, [(source, source + steps) for source in range(count - steps)])


def conv_silu(block_ref, rim_ref, weight_ref, bias_ref):
    now = block_ref[...].astype(jnp.float32)
    rim = rim_ref[...].astype(jnp.float32)
    row = lax.broadcasted_iota(jnp.int32, rim.shape, 0)
    total = bias_ref[...] + weight_ref[KERNEL - 1 : KERNEL, :] * now
    for back in range(1, KERNEL):
        moved = pltpu.roll(now, back, 0)
        top = jnp.where(row < back, pltpu.roll(rim, back, 0), moved[:RIM])
        moved = jnp.concatenate([top, moved[RIM:]], 0)
        total = total + weight_ref[KERNEL - 1 - back : KERNEL - back, :] * moved
    half = 0.5 * total
    return (half * jnp.tanh(half) + half).astype(jnp.bfloat16)


def spread(columns, pair):
    rows = columns.shape[0]
    lane = lax.broadcasted_iota(jnp.int32, (rows, 2 * P_SIZE), 1)
    return jnp.where(lane < P_SIZE, columns[:, 2 * pair : 2 * pair + 1], columns[:, 2 * pair + 1 : 2 * pair + 2])


def conv_state_kernel(
    px, pb, pc, rx, rb, rc, wx, wb, wc, bx, bb, bc, run_ref, step_ref,
    x_out, b_out, c_out, state_out,
):
    x = conv_silu(px, rx, wx, bx)
    b = conv_silu(pb, rb, wb, bb)
    x_out[...] = x
    b_out[...] = b
    c_out[...] = conv_silu(pc, rc, wc, bc)
    run = run_ref[0]
    scale = jnp.exp(run[-1:, :] - run) * step_ref[0]
    parts = []
    for pair in range(GROUP_HEADS // 2):
        columns = x[:, pair * 2 * P_SIZE : (pair + 1) * 2 * P_SIZE].astype(jnp.float32)
        parts.append((columns * spread(scale, pair)).astype(jnp.bfloat16))
    weighted = jnp.concatenate(parts, 1)
    state = lax.dot_general(
        b, weighted, (((0,), (0,)), ((), ())), preferred_element_type=jnp.float32
    ).astype(jnp.bfloat16)
    _, chunks, places, _, width = state_out.shape
    for place in range(places):
        for chunk in range(chunks):
            begin = (place * chunks + chunk) * width
            state_out[0, chunk, place] = state[:, begin : begin + width]


def scan_kernel(
    state_ref, gain_ref, x_ref, b_ref, c_ref, run_ref, run_row_ref, step_row_ref, skip_ref, out_ref,
    enter_ref, run_pair, scores_ref, within_ref, from_pair, block_send, block_recv, total_send, total_recv, enter_send, enter_recv, back_send,
    pair_gain, block_gain, block_gains, section_gain, section_gains,
    pair_sems, block_sems, total_sems, enter_sems, back_sems, pair_gain_sems, block_gain_sems, section_gain_sems,
):
    sections = lax.axis_size("sec")
    section, position = lax.axis_index("sec"), lax.axis_index("cp")
    place, side = position // 2, position % 2
    _, chunks, places, rows, width = state_ref.shape
    tokens = x_ref.shape[0]
    lane = lax.broadcasted_iota(jnp.int32, (tokens, width), 1)
    first = side == 0
    partner = (section, place * 2 + (1 - side))
    near = [lax.rem(place + step, places) for step in range(1, places)]
    line = [(section, other * 2 + side) for other in near]
    above = [(lax.rem(section + step, sections), position) for step in range(1, sections)]

    def remote(source, target, sems, at, device):
        return pltpu.make_async_remote_copy(
            src_ref=source,
            dst_ref=target,
            send_sem=sems.at[(0, *at)],
            recv_sem=sems.at[(1, *at)],
            device_id=device,
            device_id_type=pl.DeviceIdType.MESH,
        )

    barrier = pltpu.get_barrier_semaphore()
    for device in [partner, *line, *above]:
        pl.semaphore_signal(barrier, inc=1, device_id=device, device_id_type=pl.DeviceIdType.MESH)
    pl.semaphore_wait(barrier, len(line) + len(above) + 1)

    started = []

    def begin(copy):
        copy.start()
        started.append(copy)
        return copy

    pair_gain_copy = begin(remote(gain_ref.at[1 - side], pair_gain, pair_gain_sems, (0,), partner))
    pair_copies = []

    def send_pair():
        chunk = len(pair_copies)
        if chunk < chunks:
            pair_copies.append(
                begin(remote(state_ref.at[1 - side, chunk], from_pair.at[chunk], pair_sems, (chunk,), partner))
            )

    for _ in range(IN_FLIGHT):
        send_pair()

    for pair in range(HEAD_COUNT // 2):
        run_pair[pair] = run_ref[:, 2 * pair : 2 * pair + 2]
    token = lax.broadcasted_iota(jnp.int32, (tokens, tokens), 0)
    causal = token >= lax.broadcasted_iota(jnp.int32, (tokens, tokens), 1)

    def group_scores(group, carry):
        columns = pl.ds(pl.multiple_of(group * N, N), N)
        scores = lax.dot_general(
            c_ref[:, columns], b_ref[:, columns], (((1,), (1,)), ((), ())), preferred_element_type=jnp.float32
        )
        scores_ref[group] = jnp.where(causal, scores, 0.0)
        return carry

    lax.fori_loop(0, G, group_scores, 0)

    def stage_within(chunk):
        def one_place(slot, carry):
            for half in range(2):
                pair = (half * places + slot) * chunks + chunk
                columns = pl.ds(pl.multiple_of(pair * width, width), width)
                scores = scores_ref[lax.div(pair, GROUP_HEADS // 2)]
                x = x_ref[:, columns]
                run = run_pair[pair]
                run_row = run_row_ref[pair]
                step_row = step_row_ref[pair]
                found = []
                for head in range(2):
                    gap = run[:, head : head + 1] - run_row[head : head + 1, :]
                    mix = scores * jnp.exp(jnp.minimum(gap, 0.0)) * step_row[head : head + 1, :]
                    found.append(jnp.dot(mix.astype(jnp.bfloat16), x, preferred_element_type=jnp.float32))
                within_ref[pair] = (
                    jnp.where(lane < P_SIZE, found[0], found[1]) + skip_ref[pair] * x.astype(jnp.float32)
                )
            return carry

        lax.fori_loop(0, places, one_place, 0)

    def stage_finish(chunk):
        back_copies[chunk].wait_recv()

        def one_place(slot, carry):
            for half in range(2):
                pair = (half * places + slot) * chunks + chunk
                group = lax.div(pair, GROUP_HEADS // 2)
                carried = jnp.dot(
                    c_ref[:, pl.ds(pl.multiple_of(group * N, N), N)],
                    enter_ref[half, chunk, slot],
                    preferred_element_type=jnp.float32,
                )
                gain = jnp.exp(run_pair[pair])
                out_ref[:, pl.ds(pl.multiple_of(pair * width, width), width)] = (
                    within_ref[pair] + spread(gain, 0) * carried
                ).astype(jnp.bfloat16)
            return carry

        lax.fori_loop(0, places, one_place, 0)

    pair_gain_copy.wait_recv()
    block_gain[...] = gain_ref[side] * pair_gain[...]
    block_gains[place] = block_gain[place]
    block_gain_copies = [
        begin(remote(block_gain.at[other], block_gains.at[place], block_gain_sems, (step,), device))
        for step, (other, device) in enumerate(zip(near, line))
    ]
    block_copies, total_copies, enter_copies, back_copies = {}, {}, {}, {}
    section_gain_copies = []

    def pair_order(chunk, slot):
        own = state_ref[side, chunk, slot].astype(jnp.float32)
        other = from_pair[chunk, slot].astype(jnp.float32)
        return own, other

    def stage_block(chunk):
        pair_copies[chunk].wait_recv()
        send_pair()
        for slot in range(places):
            own, other = pair_order(chunk, slot)
            early, late = jnp.where(first, own, other), jnp.where(first, other, own)
            late_gain = jnp.where(first, pair_gain[slot, chunk], gain_ref[side, slot, chunk])
            block_send[chunk, slot] = (late_gain * early + late).astype(jnp.bfloat16)
        block_recv[chunk, place] = block_send[chunk, place]
        block_copies[chunk] = [
            begin(remote(block_send.at[chunk, other], block_recv.at[chunk, place], block_sems, (chunk, step), device))
            for step, (other, device) in enumerate(zip(near, line))
        ]

    def stage_total(chunk):
        if chunk == 0:
            for copy in block_gain_copies:
                copy.wait_recv()
            product = block_gains[0]
            for slot in range(1, places):
                product = product * block_gains[slot]
            section_gain[...] = product
            section_gains[section] = product
            for step, device in enumerate(above):
                section_gain_copies.append(
                    begin(remote(section_gain, section_gains.at[section], section_gain_sems, (step,), device))
                )
        for copy in block_copies[chunk]:
            copy.wait_recv()
        total = block_recv[chunk, 0].astype(jnp.float32)
        for slot in range(1, places):
            total = block_gains[slot, chunk] * total + block_recv[chunk, slot].astype(jnp.float32)
        total = total.astype(jnp.bfloat16)
        total_send[chunk] = total
        total_recv[chunk, section] = total
        total_copies[chunk] = [
            begin(remote(total_send.at[chunk], total_recv.at[chunk, section], total_sems, (chunk, step), device))
            for step, device in enumerate(above)
        ]

    def stage_enter(chunk):
        if chunk == 0:
            for copy in section_gain_copies:
                copy.wait_recv()
        for copy in total_copies[chunk]:
            copy.wait_recv()
        now = jnp.zeros((rows, width), jnp.float32)
        for other in range(sections - 1):
            later = section_gains[other, chunk] * now + total_recv[chunk, other].astype(jnp.float32)
            now = jnp.where(other < section, later, now)
        for slot in range(places):
            enter_send[chunk, slot] = now.astype(jnp.bfloat16)
            if slot < places - 1:
                now = block_gains[slot, chunk] * now + block_recv[chunk, slot].astype(jnp.float32)
        enter_recv[chunk, place] = enter_send[chunk, place]
        enter_copies[chunk] = [
            begin(remote(enter_send.at[chunk, other], enter_recv.at[chunk, place], enter_sems, (chunk, step), device))
            for step, (other, device) in enumerate(zip(near, line))
        ]

    def stage_back(chunk):
        for copy in enter_copies[chunk]:
            copy.wait_recv()
        for slot in range(places):
            own, other = pair_order(chunk, slot)
            early = jnp.where(first, own, other)
            early_gain = jnp.where(first, gain_ref[side, slot, chunk], pair_gain[slot, chunk])
            into_block = enter_recv[chunk, slot]
            into_late = (early_gain * into_block.astype(jnp.float32) + early).astype(jnp.bfloat16)
            enter_ref[side, chunk, slot] = jnp.where(first, into_block, into_late)
            back_send[chunk, slot] = jnp.where(first, into_late, into_block)
        back_copies[chunk] = begin(
            remote(back_send.at[chunk], enter_ref.at[side, chunk], back_sems, (chunk,), partner)
        )

    plan = ((stage_block, 0), (stage_within, -1), (stage_total, 1), (stage_enter, 2), (stage_back, 3), (stage_finish, 4))
    stage_within(0)
    for turn in range(chunks + 4):
        for stage, lag in plan:
            if 0 <= turn - lag < chunks:
                stage(turn - lag)
    for copy in started:
        copy.wait_send()


def params():
    return pltpu.CompilerParams(vmem_limit_bytes=VMEM_LIMIT)


def per_device(projected, conv_weight, conv_bias, step_size, log_decay, skip_gain):
    sections = lax.axis_size("sec")
    places = lax.axis_size("cp") // 2
    rows = projected.shape[0]
    place_cols = WIDTH_X // 2 // places
    width = 2 * P_SIZE
    chunks = place_cols // width
    pairs = HEAD_COUNT // 2
    group_places = GROUP_COLS // place_cols
    half_groups = G // 2
    rim = passed_along(projected[rows - RIM :], ("sec", "cp"), 1)
    lower = jnp.tril(jnp.ones((rows, rows), jnp.bfloat16))
    running = jnp.dot(lower, log_decay, preferred_element_type=jnp.float32)
    run_row = running.T.reshape(pairs, 2, rows)
    run_cols = running.reshape(rows, G, GROUP_HEADS).transpose(1, 0, 2)
    steps_f = step_size.astype(jnp.float32)
    step_row = steps_f.T.reshape(pairs, 2, rows)
    step_cols = steps_f.reshape(rows, G, GROUP_HEADS).transpose(1, 0, 2)
    skip_cols = jnp.repeat(skip_gain, P_SIZE).reshape(pairs, 1, width)
    bias = conv_bias[None]
    gain = jnp.repeat(jnp.exp(running[rows - 1]), P_SIZE).reshape(2, places, chunks, 1, width)

    def spec(height, cols, first):
        return pl.BlockSpec((height, cols), lambda g: (0, first + g))

    def three(height):
        return [spec(height, GROUP_COLS, 0), spec(height, N, WIDTH_X // N), spec(height, N, WIDTH_X // N + G)]

    group_cols = pl.BlockSpec((1, rows, GROUP_HEADS), lambda g: (g, 0, 0))
    piece_spec = pl.BlockSpec(
        (1, chunks, group_places, N, width), lambda g: (g // half_groups, 0, g % half_groups, 0, 0)
    )
    state_shape = jax.ShapeDtypeStruct((2, chunks, places, N, width), jnp.bfloat16)
    x, b, c, state = pl.pallas_call(
        conv_state_kernel,
        grid=(G,),
        in_specs=three(rows) + three(RIM) + three(KERNEL) + three(1) + [group_cols, group_cols],
        out_specs=[spec(rows, GROUP_COLS, 0), spec(rows, N, 0), spec(rows, N, 0), piece_spec],
        out_shape=[
            jax.ShapeDtypeStruct((rows, WIDTH_X), jnp.bfloat16),
            jax.ShapeDtypeStruct((rows, G * N), jnp.bfloat16),
            jax.ShapeDtypeStruct((rows, G * N), jnp.bfloat16),
            state_shape,
        ],
        compiler_params=params(),
        name="conv_state",
    )(*([projected] * 3), *([rim] * 3), *([conv_weight] * 3), *([bias] * 3), run_cols, step_cols)
    whole = pl.BlockSpec(memory_space=pltpu.VMEM)

    def held(*shape):
        return pltpu.VMEM((*shape, N, width), jnp.bfloat16)

    def gains(*shape):
        return pltpu.VMEM((*shape, chunks, 1, width), jnp.float32)

    def sems(*shape):
        return pltpu.SemaphoreType.DMA((2, *shape))

    return pl.pallas_call(
        scan_kernel,
        in_specs=[whole] * 9,
        out_specs=whole,
        out_shape=jax.ShapeDtypeStruct((rows, WIDTH_X), jnp.bfloat16),
        scratch_shapes=[
            held(2, chunks, places),
            pltpu.VMEM((pairs, rows, 2), jnp.float32),
            pltpu.VMEM((G, rows, rows), jnp.float32),
            pltpu.VMEM((pairs, rows, width), jnp.float32),
            held(chunks, places),
            held(chunks, places),
            held(chunks, places),
            held(chunks),
            held(chunks, sections),
            held(chunks, places),
            held(chunks, places),
            held(chunks, places),
            gains(places),
            gains(places),
            gains(places),
            gains(),
            gains(sections),
            sems(chunks),
            sems(chunks, places - 1),
            sems(chunks, sections - 1),
            sems(chunks, places - 1),
            sems(chunks),
            sems(1),
            sems(places - 1),
            sems(sections - 1),
        ],
        compiler_params=pltpu.CompilerParams(
            vmem_limit_bytes=VMEM_LIMIT, collective_id=0, has_side_effects=True
        ),
        name="state_scan",
    )(state, gain, x, b, c, running, run_row, step_row, skip_cols)


def solution(mesh):
    in_specs = (
        P(("sec", "cp"), None),
        P(),
        P(),
        P(("sec", "cp"), None),
        P(("sec", "cp"), None),
        P(),
    )
    out_specs = P(("sec", "cp"), None)
    return jax.shard_map(
        per_device, mesh=mesh, in_specs=in_specs, out_specs=out_specs, check_vma=False
    )
```

```python
import functools
import jax
import jax.numpy as jnp
from jax import lax
from jax.experimental import pallas as pl
from jax.experimental.pallas import tpu as pltpu
from jax.sharding import PartitionSpec as P

HEAD_COUNT = 128
P_SIZE = 64
N = 128
G = 8
KERNEL = 4
GROUP_HEADS = HEAD_COUNT // G
GROUP_COLS = GROUP_HEADS * P_SIZE
WIDTH_X = HEAD_COUNT * P_SIZE
RIM = 8
VMEM_LIMIT = 48 * 1024 * 1024


def passed_along(value, axis, steps):
    count = lax.axis_size(axis)
    return lax.ppermute(value, axis, [(source, source + steps) for source in range(count - steps)])


def conv_silu(block_ref, rim_ref, weight_ref, bias_ref):
    now = block_ref[...].astype(jnp.float32)
    rim = rim_ref[...].astype(jnp.float32)
    row = lax.broadcasted_iota(jnp.int32, rim.shape, 0)
    total = bias_ref[...] + weight_ref[KERNEL - 1 : KERNEL, :] * now
    for back in range(1, KERNEL):
        moved = pltpu.roll(now, back, 0)
        top = jnp.where(row < back, pltpu.roll(rim, back, 0), moved[:RIM])
        moved = jnp.concatenate([top, moved[RIM:]], 0)
        total = total + weight_ref[KERNEL - 1 - back : KERNEL - back, :] * moved
    return (total / (1.0 + jnp.exp(-total))).astype(jnp.bfloat16)


def spread(columns, pair):
    rows = columns.shape[0]
    lane = lax.broadcasted_iota(jnp.int32, (rows, 2 * P_SIZE), 1)
    return jnp.where(lane < P_SIZE, columns[:, 2 * pair : 2 * pair + 1], columns[:, 2 * pair + 1 : 2 * pair + 2])


def conv_state_kernel(
    px, pb, pc, rx, rb, rc, wx, wb, wc, bx, bb, bc, run_ref, step_ref,
    x_out, b_out, c_out, state_out,
):
    x = conv_silu(px, rx, wx, bx)
    b = conv_silu(pb, rb, wb, bb)
    x_out[...] = x
    b_out[...] = b
    c_out[...] = conv_silu(pc, rc, wc, bc)
    run = run_ref[0]
    scale = jnp.exp(run[-1:, :] - run) * step_ref[0]
    parts = []
    for pair in range(GROUP_HEADS // 2):
        columns = x[:, pair * 2 * P_SIZE : (pair + 1) * 2 * P_SIZE].astype(jnp.float32)
        parts.append((columns * spread(scale, pair)).astype(jnp.bfloat16))
    weighted = jnp.concatenate(parts, 1)
    state = lax.dot_general(
        b, weighted, (((0,), (0,)), ((), ())), preferred_element_type=jnp.float32
    ).astype(jnp.bfloat16)
    _, chunks, places, _, width = state_out.shape
    for place in range(places):
        for chunk in range(chunks):
            begin = (place * chunks + chunk) * width
            state_out[0, chunk, place] = state[:, begin : begin + width]


def scan_kernel(
    state_ref, gain_ref, x_ref, b_ref, c_ref, run_ref, run_row_ref, step_row_ref, skip_ref, out_ref,
    enter_ref, run_pair, scores_ref, within_ref, from_pair, block_send, block_recv, total_send, total_recv, enter_send, enter_recv, back_send,
    pair_gain, block_gain, block_gains, section_gain, section_gains,
    pair_sems, block_sems, total_sems, enter_sems, back_sems, pair_gain_sems, block_gain_sems, section_gain_sems,
):
    sections = lax.axis_size("sec")
    section, position = lax.axis_index("sec"), lax.axis_index("cp")
    place, side = position // 2, position % 2
    _, chunks, places, rows, width = state_ref.shape
    tokens = x_ref.shape[0]
    lane = lax.broadcasted_iota(jnp.int32, (tokens, width), 1)
    first = side == 0
    partner = (section, place * 2 + (1 - side))
    near = [lax.rem(place + step, places) for step in range(1, places)]
    line = [(section, other * 2 + side) for other in near]
    above = [(lax.rem(section + step, sections), position) for step in range(1, sections)]

    def remote(source, target, sems, at, device):
        return pltpu.make_async_remote_copy(
            src_ref=source,
            dst_ref=target,
            send_sem=sems.at[(0, *at)],
            recv_sem=sems.at[(1, *at)],
            device_id=device,
            device_id_type=pl.DeviceIdType.MESH,
        )

    barrier = pltpu.get_barrier_semaphore()
    for device in [partner, *line, *above]:
        pl.semaphore_signal(barrier, inc=1, device_id=device, device_id_type=pl.DeviceIdType.MESH)
    pl.semaphore_wait(barrier, len(line) + len(above) + 1)

    started = []

    def begin(copy):
        copy.start()
        started.append(copy)
        return copy

    pair_gain_copy = begin(remote(gain_ref.at[1 - side], pair_gain, pair_gain_sems, (0,), partner))
    pair_copies = [
        begin(remote(state_ref.at[1 - side, chunk], from_pair.at[chunk], pair_sems, (chunk,), partner))
        for chunk in range(chunks)
    ]

    for pair in range(HEAD_COUNT // 2):
        run_pair[pair] = run_ref[:, 2 * pair : 2 * pair + 2]
    token = lax.broadcasted_iota(jnp.int32, (tokens, tokens), 0)
    causal = token >= lax.broadcasted_iota(jnp.int32, (tokens, tokens), 1)

    def group_scores(group, carry):
        columns = pl.ds(pl.multiple_of(group * N, N), N)
        scores = lax.dot_general(
            c_ref[:, columns], b_ref[:, columns], (((1,), (1,)), ((), ())), preferred_element_type=jnp.float32
        )
        scores_ref[group] = jnp.where(causal, scores, 0.0)
        return carry

    lax.fori_loop(0, G, group_scores, 0)

    def stage_within(chunk):
        def one_place(slot, carry):
            for half in range(2):
                pair = (half * places + slot) * chunks + chunk
                columns = pl.ds(pl.multiple_of(pair * width, width), width)
                scores = scores_ref[lax.div(pair, GROUP_HEADS // 2)]
                x = x_ref[:, columns]
                run = run_pair[pair]
                run_row = run_row_ref[pair]
                step_row = step_row_ref[pair]
                found = []
                for head in range(2):
                    gap = run[:, head : head + 1] - run_row[head : head + 1, :]
                    mix = scores * jnp.exp(jnp.minimum(gap, 0.0)) * step_row[head : head + 1, :]
                    found.append(jnp.dot(mix.astype(jnp.bfloat16), x, preferred_element_type=jnp.float32))
                within_ref[pair] = (
                    jnp.where(lane < P_SIZE, found[0], found[1]) + skip_ref[pair] * x.astype(jnp.float32)
                )
            return carry

        lax.fori_loop(0, places, one_place, 0)

    def stage_finish(chunk):
        back_copies[chunk].wait_recv()

        def one_place(slot, carry):
            for half in range(2):
                pair = (half * places + slot) * chunks + chunk
                group = lax.div(pair, GROUP_HEADS // 2)
                carried = jnp.dot(
                    c_ref[:, pl.ds(pl.multiple_of(group * N, N), N)],
                    enter_ref[half, chunk, slot],
                    preferred_element_type=jnp.float32,
                )
                gain = jnp.exp(run_pair[pair])
                out_ref[:, pl.ds(pl.multiple_of(pair * width, width), width)] = (
                    within_ref[pair] + spread(gain, 0) * carried
                ).astype(jnp.bfloat16)
            return carry

        lax.fori_loop(0, places, one_place, 0)

    pair_gain_copy.wait_recv()
    block_gain[...] = gain_ref[side] * pair_gain[...]
    block_gains[place] = block_gain[place]
    block_gain_copies = [
        begin(remote(block_gain.at[other], block_gains.at[place], block_gain_sems, (step,), device))
        for step, (other, device) in enumerate(zip(near, line))
    ]
    block_copies, total_copies, enter_copies, back_copies = {}, {}, {}, {}
    section_gain_copies = []

    def pair_order(chunk, slot):
        own = state_ref[side, chunk, slot].astype(jnp.float32)
        other = from_pair[chunk, slot].astype(jnp.float32)
        return own, other

    def stage_block(chunk):
        pair_copies[chunk].wait_recv()
        for slot in range(places):
            own, other = pair_order(chunk, slot)
            early, late = jnp.where(first, own, other), jnp.where(first, other, own)
            late_gain = jnp.where(first, pair_gain[slot, chunk], gain_ref[side, slot, chunk])
            block_send[chunk, slot] = (late_gain * early + late).astype(jnp.bfloat16)
        block_recv[chunk, place] = block_send[chunk, place]
        block_copies[chunk] = [
            begin(remote(block_send.at[chunk, other], block_recv.at[chunk, place], block_sems, (chunk, step), device))
            for step, (other, device) in enumerate(zip(near, line))
        ]

    def stage_total(chunk):
        if chunk == 0:
            for copy in block_gain_copies:
                copy.wait_recv()
            product = block_gains[0]
            for slot in range(1, places):
                product = product * block_gains[slot]
            section_gain[...] = product
            section_gains[section] = product
            for step, device in enumerate(above):
                section_gain_copies.append(
                    begin(remote(section_gain, section_gains.at[section], section_gain_sems, (step,), device))
                )
        for copy in block_copies[chunk]:
            copy.wait_recv()
        total = block_recv[chunk, 0].astype(jnp.float32)
        for slot in range(1, places):
            total = block_gains[slot, chunk] * total + block_recv[chunk, slot].astype(jnp.float32)
        total = total.astype(jnp.bfloat16)
        total_send[chunk] = total
        total_recv[chunk, section] = total
        total_copies[chunk] = [
            begin(remote(total_send.at[chunk], total_recv.at[chunk, section], total_sems, (chunk, step), device))
            for step, device in enumerate(above)
        ]

    def stage_enter(chunk):
        if chunk == 0:
            for copy in section_gain_copies:
                copy.wait_recv()
        for copy in total_copies[chunk]:
            copy.wait_recv()
        now = jnp.zeros((rows, width), jnp.float32)
        for other in range(sections - 1):
            later = section_gains[other, chunk] * now + total_recv[chunk, other].astype(jnp.float32)
            now = jnp.where(other < section, later, now)
        for slot in range(places):
            enter_send[chunk, slot] = now.astype(jnp.bfloat16)
            if slot < places - 1:
                now = block_gains[slot, chunk] * now + block_recv[chunk, slot].astype(jnp.float32)
        enter_recv[chunk, place] = enter_send[chunk, place]
        enter_copies[chunk] = [
            begin(remote(enter_send.at[chunk, other], enter_recv.at[chunk, place], enter_sems, (chunk, step), device))
            for step, (other, device) in enumerate(zip(near, line))
        ]

    def stage_back(chunk):
        for copy in enter_copies[chunk]:
            copy.wait_recv()
        for slot in range(places):
            own, other = pair_order(chunk, slot)
            early = jnp.where(first, own, other)
            early_gain = jnp.where(first, gain_ref[side, slot, chunk], pair_gain[slot, chunk])
            into_block = enter_recv[chunk, slot]
            into_late = (early_gain * into_block.astype(jnp.float32) + early).astype(jnp.bfloat16)
            enter_ref[side, chunk, slot] = jnp.where(first, into_block, into_late)
            back_send[chunk, slot] = jnp.where(first, into_late, into_block)
        back_copies[chunk] = begin(
            remote(back_send.at[chunk], enter_ref.at[side, chunk], back_sems, (chunk,), partner)
        )

    plan = ((stage_back, 3), (stage_enter, 2), (stage_total, 1), (stage_block, 0), (stage_within, 0), (stage_finish, 4))
    for turn in range(chunks + 4):
        for stage, lag in plan:
            if 0 <= turn - lag < chunks:
                stage(turn - lag)
    for copy in started:
        copy.wait_send()


def params():
    return pltpu.CompilerParams(vmem_limit_bytes=VMEM_LIMIT)


def per_device(projected, conv_weight, conv_bias, step_size, log_decay, skip_gain):
    sections = lax.axis_size("sec")
    places = lax.axis_size("cp") // 2
    rows = projected.shape[0]
    place_cols = WIDTH_X // 2 // places
    width = 2 * P_SIZE
    chunks = place_cols // width
    pairs = HEAD_COUNT // 2
    group_places = GROUP_COLS // place_cols
    half_groups = G // 2
    rim = passed_along(projected[rows - RIM :], ("sec", "cp"), 1)
    lower = jnp.tril(jnp.ones((rows, rows), jnp.bfloat16))
    running = jnp.dot(lower, log_decay, preferred_element_type=jnp.float32)
    run_row = running.T.reshape(pairs, 2, rows)
    run_cols = running.reshape(rows, G, GROUP_HEADS).transpose(1, 0, 2)
    steps_f = step_size.astype(jnp.float32)
    step_row = steps_f.T.reshape(pairs, 2, rows)
    step_cols = steps_f.reshape(rows, G, GROUP_HEADS).transpose(1, 0, 2)
    skip_cols = jnp.repeat(skip_gain, P_SIZE).reshape(pairs, 1, width)
    bias = conv_bias[None]
    gain = jnp.repeat(jnp.exp(running[rows - 1]), P_SIZE).reshape(2, places, chunks, 1, width)

    def spec(height, cols, first):
        return pl.BlockSpec((height, cols), lambda g: (0, first + g))

    def three(height):
        return [spec(height, GROUP_COLS, 0), spec(height, N, WIDTH_X // N), spec(height, N, WIDTH_X // N + G)]

    group_cols = pl.BlockSpec((1, rows, GROUP_HEADS), lambda g: (g, 0, 0))
    piece_spec = pl.BlockSpec(
        (1, chunks, group_places, N, width), lambda g: (g // half_groups, 0, g % half_groups, 0, 0)
    )
    state_shape = jax.ShapeDtypeStruct((2, chunks, places, N, width), jnp.bfloat16)
    x, b, c, state = pl.pallas_call(
        conv_state_kernel,
        grid=(G,),
        in_specs=three(rows) + three(RIM) + three(KERNEL) + three(1) + [group_cols, group_cols],
        out_specs=[spec(rows, GROUP_COLS, 0), spec(rows, N, 0), spec(rows, N, 0), piece_spec],
        out_shape=[
            jax.ShapeDtypeStruct((rows, WIDTH_X), jnp.bfloat16),
            jax.ShapeDtypeStruct((rows, G * N), jnp.bfloat16),
            jax.ShapeDtypeStruct((rows, G * N), jnp.bfloat16),
            state_shape,
        ],
        compiler_params=params(),
        name="conv_state",
    )(*([projected] * 3), *([rim] * 3), *([conv_weight] * 3), *([bias] * 3), run_cols, step_cols)
    whole = pl.BlockSpec(memory_space=pltpu.VMEM)

    def held(*shape):
        return pltpu.VMEM((*shape, N, width), jnp.bfloat16)

    def gains(*shape):
        return pltpu.VMEM((*shape, chunks, 1, width), jnp.float32)

    def sems(*shape):
        return pltpu.SemaphoreType.DMA((2, *shape))

    return pl.pallas_call(
        scan_kernel,
        in_specs=[whole] * 9,
        out_specs=whole,
        out_shape=jax.ShapeDtypeStruct((rows, WIDTH_X), jnp.bfloat16),
        scratch_shapes=[
            held(2, chunks, places),
            pltpu.VMEM((pairs, rows, 2), jnp.float32),
            pltpu.VMEM((G, rows, rows), jnp.float32),
            pltpu.VMEM((pairs, rows, width), jnp.float32),
            held(chunks, places),
            held(chunks, places),
            held(chunks, places),
            held(chunks),
            held(chunks, sections),
            held(chunks, places),
            held(chunks, places),
            held(chunks, places),
            gains(places),
            gains(places),
            gains(places),
            gains(),
            gains(sections),
            sems(chunks),
            sems(chunks, places - 1),
            sems(chunks, sections - 1),
            sems(chunks, places - 1),
            sems(chunks),
            sems(1),
            sems(places - 1),
            sems(sections - 1),
        ],
        compiler_params=pltpu.CompilerParams(
            vmem_limit_bytes=VMEM_LIMIT, collective_id=0, has_side_effects=True
        ),
        name="state_scan",
    )(state, gain, x, b, c, running, run_row, step_row, skip_cols)


def solution(mesh):
    in_specs = (
        P(("sec", "cp"), None),
        P(),
        P(),
        P(("sec", "cp"), None),
        P(("sec", "cp"), None),
        P(),
    )
    out_specs = P(("sec", "cp"), None)
    return jax.shard_map(
        per_device, mesh=mesh, in_specs=in_specs, out_specs=out_specs, check_vma=False
    )
```
